32 devices in a mesh: tm: 8 (over z, x), space: 4 (over y, core).
Axes of the slice: x: 2, y: 2, z: 4, core: 2. Of those that a mesh axis runs over, the one named last changes fastest.
Arguments:
- coarse_states: float32 [8, 6, 64, 512], P('tm', None, 'space'), may hold values from -6 to 6
- initial_condition: float32 [6, 64, 512], P(None, 'space'), may hold values from -6 to 6
- base_velocity: float32 [64, 512], P('space'), may hold values from 0.5 to 2
- base_shear: float32 [64, 512], P('space'), may hold values from -1 to 1
- base_stress: float32 [2, 64, 512], P(None, 'space'), may hold values from -1 to 1
- relax_rate: float32 [64, 512], P('space'), may hold values from 0.05 to 2
Outputs:
- corrected: float32 [8, 6, 64, 512], P('tm', None, 'space')
- residual: float32 [8, 6, 64, 512], P('tm', None, 'space')
The draws below stay inside these ranges and needn't reach their ends.
All inputs are finite; a program needn't handle non-finite values.
Results may differ from the reference program's by a relative error of at most 0.00002.
Values sent between devices are 32-bit elements; how exact they have to be, the bound alone decides.
A program may use at most 64 MiB of HBM per device.

```python
import math
import jax
import jax.numpy as jnp
from jax import lax

NY = 512
STEPS_SLAB = 8
CHAIN = 4
SLABS = 8
NX = 64


def shard_levels(stream_key, dims, split, smallest, largest):
    def one(dim, shards_of):
        steps = jax.random.uniform(jax.random.fold_in(jax.random.fold_in(stream_key, 6), dim), (shards_of,), jnp.float32, smallest / len(split), largest / len(split))
        return jnp.repeat(jnp.exp(steps), dims[dim] // shards_of).reshape((-1,) + (1,) * (len(dims) - dim - 1))

    loudness = one(*split[0])
    for cut in split[1:]:
        loudness = loudness * one(*cut)
    return loudness


def scatter_about(stream_key, dims, deviation, most, split=(), kind=jnp.bfloat16):
    entries = deviation * jax.random.normal(stream_key, dims, jnp.float32)
    if split:
        entries = entries * shard_levels(stream_key, dims, split, -0.22, 0.18)
    return jnp.clip(entries, -most, most).astype(kind)


def setup_inputs(seed: int = 0) -> dict:
    seeds = jax.random.split(jax.random.key(seed), 7)
    return {
        "coarse_states": scatter_about(seeds[0], (SLABS, 6, NX, NY), 1.0, 6.0, ((0, 8), (2, 4)), jnp.float32),
        "initial_condition": scatter_about(seeds[1], (6, NX, NY), 1.0, 6.0, ((1, 4),), jnp.float32),
        "base_velocity": jnp.clip(0.5 + 1.5 * jax.random.uniform(seeds[2], (NX, NY), jnp.float32) ** shard_levels(seeds[2], (NX, NY), ((0, 4),), -0.2, 0.2), 0.5, 2.0),
        "base_shear": jnp.clip(jax.random.uniform(seeds[3], (NX, NY), jnp.float32, -1.0, 1.0) * shard_levels(seeds[3], (NX, NY), ((0, 4),), -0.4, 0.0), -1.0, 1.0),
        "base_stress": jnp.clip(jax.random.uniform(seeds[4], (2, NX, NY), jnp.float32, -1.0, 1.0) * shard_levels(seeds[4], (2, NX, NY), ((1, 4),), -0.4, 0.0), -1.0, 1.0),
        "relax_rate": jnp.clip(jnp.exp(math.log(2.0) - 3.6888794 * jax.random.uniform(seeds[5], (NX, NY), jnp.float32) ** shard_levels(seeds[5], (NX, NY), ((0, 4),), -0.2, 0.2)), 0.05, 2.0),
    }


fine_step = 0.1
viscosity = 0.5
sound_sq = 1.0


def advance(extended, coef_rows, time_step):
    padded = jnp.pad(extended, ((0, 0), (0, 0), (1, 1)))
    center = padded[:, 1:-1, 1:-1]
    x_plus = padded[:, 2:, 1:-1]
    x_minus = padded[:, :-2, 1:-1]
    y_plus = padded[:, 1:-1, 2:]
    y_minus = padded[:, 1:-1, :-2]
    grad_x = 0.5 * (x_plus - x_minus)
    grad_y = 0.5 * (y_plus - y_minus)
    smooth = viscosity * (x_plus + x_minus + y_plus + y_minus - 4.0 * center)
    base_u = coef_rows[0]
    shear = coef_rows[1]
    stress_xx = coef_rows[2]
    stress_xy = coef_rows[3]
    rate = coef_rows[4]
    vel_v = center[1]
    str_a = center[3]
    str_b = center[4]
    str_c = center[5]
    tend_u = -base_u * grad_x[0] - shear * vel_v - grad_x[2] + grad_x[3] + grad_y[4] + smooth[0]
    tend_v = -base_u * grad_x[1] - grad_y[2] + grad_x[4] + grad_y[5] + smooth[1]
    tend_p = -sound_sq * (grad_x[0] + grad_y[1]) + smooth[2]
    tend_a = (-base_u * grad_x[3] + 2.0 * shear * str_b + 2.0 * (stress_xx * grad_x[0] + stress_xy * grad_y[0])
              + 2.0 * rate * grad_x[0] - rate * str_a + smooth[3])
    tend_b = (-base_u * grad_x[4] + shear * str_c + stress_xy * grad_x[0] + stress_xx * grad_x[1] + stress_xy * grad_y[1]
              + rate * (grad_y[0] + grad_x[1]) - rate * str_b + smooth[4])
    tend_c = -base_u * grad_x[5] + 2.0 * stress_xy * grad_x[1] + 2.0 * rate * grad_y[1] - rate * str_c + smooth[5]
    tendency = jnp.stack([tend_u, tend_v, tend_p, tend_a, tend_b, tend_c], 0)
    return center + time_step * tendency


def one_step(field, coefficients, time_step):
    extended = jnp.concatenate([field[:, -1:], field, field[:, :1]], 1)
    return advance(extended, coefficients, time_step)


def reference(coarse_states, initial_condition, base_velocity, base_shear, base_stress, relax_rate):
    coefficients = jnp.concatenate([base_velocity[None], base_shear[None], base_stress, relax_rate[None]], 0)
    coarse_dt = STEPS_SLAB * fine_step / 4.0

    def whole_slab(field):
        for repeat in range(STEPS_SLAB):
            field = one_step(field, coefficients, fine_step)
        return field

    def coarse(field):
        for repeat in range(4):
            field = one_step(field, coefficients, coarse_dt)
        return field

    propagated = lax.map(whole_slab, coarse_states)
    cpoint = jnp.concatenate([coarse_states[:1], propagated[:-1]], 0)
    ahead = lax.map(whole_slab, cpoint)
    zero_slab = jnp.zeros_like(cpoint[:1])
    first_residual = (initial_condition - cpoint[0])[None]
    residual = jnp.concatenate([first_residual, ahead[:-1] - cpoint[1:]], 0)
    correction = residual
    for repeat in range(CHAIN - 1):
        moved = jnp.concatenate([zero_slab, correction[:-1]], 0)
        correction = residual + lax.map(coarse, moved)
    return cpoint + correction, residual
```

```python
import functools

import jax
import jax.numpy as jnp
from jax import lax
from jax.experimental import pallas as pl
from jax.experimental.pallas import tpu as pltpu
from jax.sharding import PartitionSpec as P

STEPS_SLAB = 8
FINE = 0.1
NU = 0.5
SOUND_SQ = 1.0
COARSE = STEPS_SLAB * FINE / 4.0

MESH = pl.DeviceIdType.MESH
f32 = jnp.float32

ROWS = 16
TOP = 16
HEIGHT = 48
BLOCKS = 4
N_COEF = 10


def kernel(
    n_tm, n_space,
    cs, ini, bv, bs, bp, rr,
    corr, resid,
    F, K, X, HX, HB, HR, HY, PR, bst, brecv, ast, arecv, rst, cst, crecv, yst, est, erecv,
    ssem, rsem,
):
    tm = lax.axis_index("tm")
    sp = lax.axis_index("space")
    up = lax.rem(sp + n_space - 1, n_space)
    down = lax.rem(sp + 1, n_space)

    def cols(j):
        return pl.ds(128 * j, 128)

    barrier = pltpu.get_barrier_semaphore()
    pl.semaphore_signal(barrier, inc=1, device_id={"space": up}, device_id_type=MESH)
    pl.semaphore_signal(barrier, inc=1, device_id={"space": down}, device_id_type=MESH)
    for d in (1, 2, n_tm - 2, n_tm - 1):
        pl.semaphore_signal(barrier, inc=1, device_id={"tm": lax.rem(tm + d, n_tm)}, device_id_type=MESH)

    for c in range(6):
        X[c] = cs[0, c]
    X[6] = bv[...]
    X[7] = bs[...]
    X[8] = bp[0]
    X[9] = bp[1]
    X[10] = rr[...]
    zero8 = jnp.zeros((8, 128), f32)
    for b in range(2):
        for c in range(6):
            for j in range(BLOCKS):
                F[b, c, j, 0:8, :] = zero8
                F[b, c, j, 40:48, :] = zero8
    for b in range(2):
        for c in range(N_COEF):
            for j in range(BLOCKS):
                K[b, c, j, 0:8, :] = zero8
                K[b, c, j, 40:48, :] = zero8

    pl.semaphore_wait(barrier, 6)

    def halo(i, to_up, to_down, buf):
        a = pltpu.make_async_remote_copy(
            src_ref=to_up, dst_ref=buf.at[1], send_sem=ssem.at[2 * i], recv_sem=rsem.at[2 * i],
            device_id={"space": up}, device_id_type=MESH)
        b = pltpu.make_async_remote_copy(
            src_ref=to_down, dst_ref=buf.at[0], send_sem=ssem.at[2 * i + 1], recv_sem=rsem.at[2 * i + 1],
            device_id={"space": down}, device_id_type=MESH)
        a.start()
        b.start()
        return a, b

    def hop(i, src, dst, d):
        return pltpu.make_async_remote_copy(
            src_ref=src, dst_ref=dst, send_sem=ssem.at[8 + i], recv_sem=rsem.at[8 + i],
            device_id={"tm": lax.rem(tm + d, n_tm)}, device_id_type=MESH)

    def send(i, src, dst, d):
        @pl.when(tm + d < n_tm)
        def _():
            hop(i, src, dst, d).start()

    def sent(i, src, dst, d):
        @pl.when(tm + d < n_tm)
        def _():
            hop(i, src, dst, d).wait_send()

    def received(i, src, dst, d):
        @pl.when(tm >= d)
        def _():
            hop(i, src, dst, d).wait_recv()

    def set_coefs(rows, get):
        for j in range(BLOCKS):
            U, S, Pp, Q, R = [get(6 + i, j) for i in range(5)]
            for b, h in enumerate((FINE, COARSE)):
                k = 0.5 * h
                K[b, 0, j, rows, :] = k * U
                K[b, 1, j, rows, :] = h * S
                K[b, 2, j, rows, :] = (2.0 * h) * S
                K[b, 3, j, rows, :] = h * (Pp + R)
                K[b, 4, j, rows, :] = k * (Pp + R)
                K[b, 5, j, rows, :] = h * Q
                K[b, 6, j, rows, :] = k * Q
                K[b, 7, j, rows, :] = h * R
                K[b, 8, j, rows, :] = k * R
                K[b, 9, j, rows, :] = (1.0 - 4.0 * NU * h) - h * R

    def step(src, b, h, left):
        dst = 1 - src
        k = 0.5 * h
        c0 = 1.0 - 4.0 * NU * h
        c1 = NU * h
        lane = lax.broadcasted_iota(jnp.int32, (8, 128), 1)
        first = lane == 0
        last = lane == 127
        start = TOP - left
        tiles = (ROWS + 2 * left + 7) // 8

        def tile(t, carry):
            r = start + 8 * t
            here = pl.ds(r, 8)
            cen, rm, rp = {}, {}, {}

            def center(c, j):
                if (c, j) not in cen:
                    cen[c, j] = F[src, c, j, here, :]
                return cen[c, j]

            def minus(c, j):
                if j < 0:
                    return zero8
                if (c, j) not in rm:
                    rm[c, j] = pltpu.roll(center(c, j), 1, 1)
                return rm[c, j]

            def plus(c, j):
                if j >= BLOCKS:
                    return zero8
                if (c, j) not in rp:
                    rp[c, j] = pltpu.roll(center(c, j), 127, 1)
                return rp[c, j]

            for j in range(BLOCKS):
                f, dx, dy, sm = [], [], [], []
                for c in range(6):
                    xm = F[src, c, j, pl.ds(r - 1, 8), :]
                    xp = F[src, c, j, pl.ds(r + 1, 8), :]
                    ym = jnp.where(first, minus(c, j - 1), minus(c, j))
                    yp = jnp.where(last, plus(c, j + 1), plus(c, j))
                    f.append(center(c, j))
                    dx.append(xp - xm)
                    dy.append(yp - ym)
                    sm.append((xp + xm) + (yp + ym))
                kU, hS, h2S, hPR, kPR, hQ, kQ, hR, kR, d0 = [K[b, i, j, here, :] for i in range(N_COEF)]
                div = dx[0] + dy[1]
                out = [
                    c0 * f[0] + c1 * sm[0] + k * (dx[3] - dx[2] + dy[4]) - kU * dx[0] - hS * f[1],
                    c0 * f[1] + c1 * sm[1] + k * (dx[4] - dy[2] + dy[5]) - kU * dx[1],
                    c0 * f[2] + c1 * sm[2] - (k * SOUND_SQ) * div,
                    d0 * f[3] + c1 * sm[3] - kU * dx[3] + h2S * f[4] + hPR * dx[0] + hQ * dy[0],
                    d0 * f[4] + c1 * sm[4] - kU * dx[4] + hS * f[5] + kQ * div + kPR * dx[1] + kR * dy[0],
                    d0 * f[5] + c1 * sm[5] - kU * dx[5] + hQ * dx[1] + hR * dy[1],
                ]
                for c in range(6):
                    F[dst, c, j, here, :] = out[c]
            return carry

        lax.fori_loop(0, tiles, tile, 0)

    def steps(count, b, h):
        def pair(i, carry):
            step(0, b, h, count - 1 - 2 * i)
            step(1, b, h, count - 2 - 2 * i)
            return carry

        lax.fori_loop(0, count // 2, pair, 0)

    def put_halo(buf):
        for c in range(6):
            for j in range(BLOCKS):
                F[0, c, j, 8:16, :] = buf[0, c, j]
                F[0, c, j, 32:40, :] = buf[1, c, j]

    OWN = slice(TOP, TOP + ROWS)

    hx = halo(0, X.at[:, 0:8, :], X.at[:, 8:16, :], HX)
    for c in range(6):
        for j in range(BLOCKS):
            F[0, c, j, OWN, :] = X[c, :, cols(j)]
    set_coefs(OWN, lambda i, j: X[i, :, cols(j)])
    for a in hx:
        a.wait()
    for side, lo in ((0, 8), (1, 32)):
        rows = slice(lo, lo + 8)
        for c in range(6):
            for j in range(BLOCKS):
                F[0, c, j, rows, :] = HX[side, c, :, cols(j)]
        set_coefs(rows, lambda i, j: HX[side, i, :, cols(j)])
    steps(8, 0, FINE)

    for c in range(6):
        for j in range(BLOCKS):
            bst[c, j] = F[0, c, j, OWN, :]
    hb = halo(1, bst.at[:, :, 0:8, :], bst.at[:, :, 8:16, :], HB)
    send(0, bst, brecv, 1)
    for a in hb:
        a.wait()
    put_halo(HB)
    steps(8, 0, FINE)
    for c in range(6):
        for j in range(BLOCKS):
            ast[c, j] = F[0, c, j, OWN, :]
    send(1, ast, arecv, 2)

    received(0, bst, brecv, 1)
    received(1, ast, arecv, 2)

    @pl.when(tm == 0)
    def _():
        for c in range(6):
            for j in range(BLOCKS):
                brecv[c, j] = cs[0, c, :, cols(j)]
                rst[c, j] = ini[c, :, cols(j)] - cs[0, c, :, cols(j)]

    @pl.when(tm == 1)
    def _():
        for c in range(6):
            for j in range(BLOCKS):
                rst[c, j] = brecv[c, j] - brecv[c, j]

    @pl.when(tm >= 2)
    def _():
        for c in range(6):
            for j in range(BLOCKS):
                rst[c, j] = arecv[c, j] - brecv[c, j]

    for c in range(6):
        for j in range(BLOCKS):
            half = slice(4 * (j % 2), 4 * (j % 2) + 4)
            PR[0, c, j // 2, half, :] = rst[c, j, 0:4, :]
            PR[1, c, j // 2, half, :] = rst[c, j, 12:16, :]
    hr = halo(2, PR.at[0], PR.at[1], HR)
    for c in range(6):
        for j in range(BLOCKS):
            v = rst[c, j]
            resid[0, c, :, cols(j)] = v
            F[0, c, j, OWN, :] = v
    for a in hr:
        a.wait()
    for c in range(6):
        for j in range(BLOCKS):
            half = slice(4 * (j % 2), 4 * (j % 2) + 4)
            F[0, c, j, 12:16, :] = HR[0, c, j // 2, half, :]
            F[0, c, j, 32:36, :] = HR[1, c, j // 2, half, :]
    steps(4, 1, COARSE)
    for c in range(6):
        for j in range(BLOCKS):
            cst[c, j] = F[0, c, j, OWN, :]
    send(2, cst, crecv, 1)
    received(2, cst, crecv, 1)

    @pl.when(tm == 0)
    def _():
        yst[...] = rst[...]

    @pl.when(tm >= 1)
    def _():
        for c in range(6):
            for j in range(BLOCKS):
                yst[c, j] = rst[c, j] + crecv[c, j]

    hy = halo(3, yst.at[:, :, 0:8, :], yst.at[:, :, 8:16, :], HY)
    for c in range(6):
        for j in range(BLOCKS):
            F[0, c, j, OWN, :] = yst[c, j]
    for a in hy:
        a.wait()
    put_halo(HY)
    steps(8, 1, COARSE)
    for c in range(6):
        for j in range(BLOCKS):
            est[c, j] = F[0, c, j, OWN, :]
    send(3, est, erecv, 2)
    received(3, est, erecv, 2)

    @pl.when(tm < 2)
    def _():
        for c in range(6):
            for j in range(BLOCKS):
                corr[0, c, :, cols(j)] = brecv[c, j] + yst[c, j]

    @pl.when(tm >= 2)
    def _():
        for c in range(6):
            for j in range(BLOCKS):
                corr[0, c, :, cols(j)] = brecv[c, j] + (yst[c, j] + erecv[c, j])

    sent(0, bst, brecv, 1)
    sent(1, ast, arecv, 2)
    sent(2, cst, crecv, 1)
    sent(3, est, erecv, 2)


def per_device(n_tm, n_space, cs, ini, bv, bs, bp, rr):
    vmem = pl.BlockSpec(memory_space=pltpu.VMEM)
    strip = pltpu.VMEM((6, BLOCKS, ROWS, 128), f32)
    halo8 = pltpu.VMEM((2, 6, BLOCKS, 8, 128), f32)
    shape = jax.ShapeDtypeStruct(cs.shape, f32)
    return pl.pallas_call(
        functools.partial(kernel, n_tm, n_space),
        out_shape=(shape, shape),
        in_specs=[vmem] * 6,
        out_specs=(vmem, vmem),
        scratch_shapes=[
            pltpu.VMEM((2, 6, BLOCKS, HEIGHT, 128), f32),
            pltpu.VMEM((2, N_COEF, BLOCKS, HEIGHT, 128), f32),
            pltpu.VMEM((11, ROWS, 512), f32),
            pltpu.VMEM((2, 11, 8, 512), f32),
            halo8,
            pltpu.VMEM((2, 6, 2, 8, 128), f32),
            halo8,
            pltpu.VMEM((2, 6, 2, 8, 128), f32),
            strip, strip, strip, strip, strip, strip, strip, strip, strip, strip,
            pltpu.SemaphoreType.DMA((12,)),
            pltpu.SemaphoreType.DMA((12,)),
        ],
        compiler_params=pltpu.CompilerParams(
            collective_id=0, has_side_effects=True, vmem_limit_bytes=32 * 1024 * 1024
        ),
    )(cs, ini, bv, bs, bp, rr)


def solution(mesh):
    n_tm, n_space = mesh.shape["tm"], mesh.shape["space"]
    return jax.shard_map(
        functools.partial(per_device, n_tm, n_space),
        mesh=mesh,
        in_specs=(
            P("tm", None, "space", None),
            P(None, "space", None),
            P("space", None),
            P("space", None),
            P(None, "space", None),
            P("space", None),
        ),
        out_specs=(P("tm", None, "space", None), P("tm", None, "space", None)),
        check_vma=False,
    )
```

```python
import functools

import jax
import jax.numpy as jnp
from jax import lax
from jax.experimental import pallas as pl
from jax.experimental.pallas import tpu as pltpu
from jax.sharding import PartitionSpec as P

STEPS_SLAB = 8
FINE = 0.1
NU = 0.5
SOUND_SQ = 1.0
COARSE = STEPS_SLAB * FINE / 4.0

MESH = pl.DeviceIdType.MESH
f32 = jnp.float32

ROWS = 16
TOP = 16
HEIGHT = 48
BLOCKS = 4
N_COEF = 10


def kernel(
    n_tm, n_space,
    cs, ini, bv, bs, bp, rr,
    corr, resid,
    F, K, X, HX, HB, HR, HY, PR, bst, brecv, ast, arecv, rst, cst, crecv, yst, est, erecv,
    start_field, ssem, rsem, lsem,
):
    tm = lax.axis_index("tm")
    sp = lax.axis_index("space")
    up = lax.rem(sp + n_space - 1, n_space)
    down = lax.rem(sp + 1, n_space)

    def cols(j):
        return pl.ds(128 * j, 128)

    barrier = pltpu.get_barrier_semaphore()
    pl.semaphore_signal(barrier, inc=1, device_id={"space": up}, device_id_type=MESH)
    pl.semaphore_signal(barrier, inc=1, device_id={"space": down}, device_id_type=MESH)
    for d in (1, 2):
        @pl.when(tm >= d)
        def _():
            pl.semaphore_signal(barrier, inc=1, device_id={"tm": tm - d}, device_id_type=MESH)

    fetches = [
        pltpu.make_async_copy(src, dst, lsem.at[i])
        for i, (src, dst) in enumerate((
            (cs.at[0], X.at[0:6]), (bv, X.at[6]), (bs, X.at[7]), (bp, X.at[8:10]), (rr, X.at[10]), (ini, start_field),
        ))
    ]
    for a in fetches:
        a.start()

    zero8 = jnp.zeros((8, 128), f32)
    for b in range(2):
        for c in range(6):
            for j in range(BLOCKS):
                F[b, c, j, 0:8, :] = zero8
                F[b, c, j, 40:48, :] = zero8
    for b in range(2):
        for c in range(N_COEF):
            for j in range(BLOCKS):
                K[b, c, j, 0:8, :] = zero8
                K[b, c, j, 40:48, :] = zero8

    for a in fetches:
        a.wait()
    pl.semaphore_wait(barrier, 4 - tm // (n_tm - 1) - tm // (n_tm - 2))

    def exchange(i, to_up, to_down, from_up, from_down):
        a = pltpu.make_async_remote_copy(
            src_ref=to_up, dst_ref=from_down, send_sem=ssem.at[i], recv_sem=rsem.at[i],
            device_id={"space": up}, device_id_type=MESH)
        b = pltpu.make_async_remote_copy(
            src_ref=to_down, dst_ref=from_up, send_sem=ssem.at[i + 1], recv_sem=rsem.at[i + 1],
            device_id={"space": down}, device_id_type=MESH)
        a.start()
        b.start()
        return [a, b]

    def hop(i, src, dst, d, j):
        return pltpu.make_async_remote_copy(
            src_ref=src.at[:, j], dst_ref=dst.at[:, j], send_sem=ssem.at[i + j], recv_sem=rsem.at[i + j],
            device_id={"tm": lax.rem(tm + d, n_tm)}, device_id_type=MESH)

    def send(i, src, dst, d, j):
        @pl.when(tm + d < n_tm)
        def _():
            hop(i, src, dst, d, j).start()

    def sent(i, src, dst, d):
        @pl.when(tm + d < n_tm)
        def _():
            for j in range(BLOCKS):
                hop(i, src, dst, d, j).wait_send()

    def received(i, src, dst, d, j):
        @pl.when(tm >= d)
        def _():
            hop(i, src, dst, d, j).wait_recv()

    def set_coefs(rows, get):
        for j in range(BLOCKS):
            U, S, Pp, Q, R = [get(6 + i, j) for i in range(5)]
            for b, h in enumerate((FINE, COARSE)):
                k = 0.5 * h
                K[b, 0, j, rows, :] = k * U
                K[b, 1, j, rows, :] = h * S
                K[b, 2, j, rows, :] = (2.0 * h) * S
                K[b, 3, j, rows, :] = h * (Pp + R)
                K[b, 4, j, rows, :] = k * (Pp + R)
                K[b, 5, j, rows, :] = h * Q
                K[b, 6, j, rows, :] = k * Q
                K[b, 7, j, rows, :] = h * R
                K[b, 8, j, rows, :] = k * R
                K[b, 9, j, rows, :] = (1.0 - 4.0 * NU * h) - h * R

    def step(src, b, h, left, tiles):
        dst = 1 - src
        k = 0.5 * h
        c0 = 1.0 - 4.0 * NU * h
        c1 = NU * h
        lane = lax.broadcasted_iota(jnp.int32, (8, 128), 1)
        first = lane == 0
        last = lane == 127
        start = TOP - left

        def tile(t):
            r = start + 8 * t
            here = pl.ds(r, 8)
            cen, rm, rp = {}, {}, {}

            def center(c, j):
                if (c, j) not in cen:
                    cen[c, j] = F[src, c, j, here, :]
                return cen[c, j]

            def minus(c, j):
                if j < 0:
                    return zero8
                if (c, j) not in rm:
                    rm[c, j] = pltpu.roll(center(c, j), 1, 1)
                return rm[c, j]

            def plus(c, j):
                if j >= BLOCKS:
                    return zero8
                if (c, j) not in rp:
                    rp[c, j] = pltpu.roll(center(c, j), 127, 1)
                return rp[c, j]

            for j in range(BLOCKS):
                f, dx, dy, sm = [], [], [], []
                for c in range(6):
                    xm = F[src, c, j, pl.ds(r - 1, 8), :]
                    xp = F[src, c, j, pl.ds(r + 1, 8), :]
                    ym = jnp.where(first, minus(c, j - 1), minus(c, j))
                    yp = jnp.where(last, plus(c, j + 1), plus(c, j))
                    f.append(center(c, j))
                    dx.append(xp - xm)
                    dy.append(yp - ym)
                    sm.append((xp + xm) + (yp + ym))
                kU, hS, h2S, hPR, kPR, hQ, kQ, hR, kR, d0 = [K[b, i, j, here, :] for i in range(N_COEF)]
                div = dx[0] + dy[1]
                out = [
                    c0 * f[0] + c1 * sm[0] + k * (dx[3] - dx[2] + dy[4]) - kU * dx[0] - hS * f[1],
                    c0 * f[1] + c1 * sm[1] + k * (dx[4] - dy[2] + dy[5]) - kU * dx[1],
                    c0 * f[2] + c1 * sm[2] - (k * SOUND_SQ) * div,
                    d0 * f[3] + c1 * sm[3] - kU * dx[3] + h2S * f[4] + hPR * dx[0] + hQ * dy[0],
                    d0 * f[4] + c1 * sm[4] - kU * dx[4] + hS * f[5] + kQ * div + kPR * dx[1] + kR * dy[0],
                    d0 * f[5] + c1 * sm[5] - kU * dx[5] + hQ * dx[1] + hR * dy[1],
                ]
                for c in range(6):
                    F[dst, c, j, here, :] = out[c]

        for t in range(tiles):
            tile(t)

    def steps(count, b, h):
        def pairs(first, end, tiles):
            def pair(i, carry):
                step(0, b, h, count - 1 - 2 * i, tiles)
                step(1, b, h, count - 2 - 2 * i, tiles)
                return carry

            lax.fori_loop(first, end, pair, 0)

        if count > 4:
            pairs(0, (count - 4) // 2, 4)
        pairs((count - 4) // 2, count // 2, 3)

    def put_halo(buf):
        for c in range(6):
            for j in range(BLOCKS):
                F[0, c, j, 8:16, :] = buf[0, c, j]
                F[0, c, j, 32:40, :] = buf[1, c, j]

    OWN = slice(TOP, TOP + ROWS)

    BLK = range(BLOCKS)
    S_X, S_B, S_R, S_Y, S_H = 0, 2, 4, 8, 16

    hx = exchange(S_X, X.at[:, 0:8, :], X.at[:, 8:16, :], HX.at[0], HX.at[1])
    for c in range(6):
        for j in BLK:
            F[0, c, j, OWN, :] = X[c, :, cols(j)]
    set_coefs(OWN, lambda i, j: X[i, :, cols(j)])
    for a in hx:
        a.wait()
    for side, lo in ((0, 8), (1, 32)):
        rows = slice(lo, lo + 8)
        for c in range(6):
            for j in BLK:
                F[0, c, j, rows, :] = HX[side, c, :, cols(j)]
        set_coefs(rows, lambda i, j: HX[side, i, :, cols(j)])
    steps(8, 0, FINE)

    for c in range(6):
        for j in BLK:
            bst[c, j] = F[0, c, j, OWN, :]
    hb = exchange(S_B, bst.at[:, :, 0:8, :], bst.at[:, :, 8:16, :], HB.at[0], HB.at[1])
    for j in BLK:
        send(S_H, bst, brecv, 1, j)
    for a in hb:
        a.wait()
    put_halo(HB)
    steps(8, 0, FINE)
    for j in BLK:
        for c in range(6):
            ast[c, j] = F[0, c, j, OWN, :]
        send(S_H + 4, ast, arecv, 2, j)

    hr = []
    for j in BLK:
        received(S_H, bst, brecv, 1, j)
        received(S_H + 4, ast, arecv, 2, j)

        @pl.when(tm == 0)
        def _():
            for c in range(6):
                brecv[c, j] = X[c, :, cols(j)]
                rst[c, j] = start_field[c, :, cols(j)] - X[c, :, cols(j)]

        @pl.when(tm == 1)
        def _():
            for c in range(6):
                rst[c, j] = brecv[c, j] - brecv[c, j]

        @pl.when(tm >= 2)
        def _():
            for c in range(6):
                rst[c, j] = arecv[c, j] - brecv[c, j]

        half = slice(4 * (j % 2), 4 * (j % 2) + 4)
        for c in range(6):
            PR[0, c, j // 2, half, :] = rst[c, j, 0:4, :]
            PR[1, c, j // 2, half, :] = rst[c, j, 12:16, :]
        if j % 2:
            p = j // 2
            hr += exchange(S_R + 2 * p, PR.at[0, :, p], PR.at[1, :, p], HR.at[0, :, p], HR.at[1, :, p])
    for c in range(6):
        for j in BLK:
            v = rst[c, j]
            resid[0, c, :, cols(j)] = v
            F[0, c, j, OWN, :] = v
    for a in hr:
        a.wait()
    for c in range(6):
        for j in BLK:
            half = slice(4 * (j % 2), 4 * (j % 2) + 4)
            F[0, c, j, 12:16, :] = HR[0, c, j // 2, half, :]
            F[0, c, j, 32:36, :] = HR[1, c, j // 2, half, :]
    steps(4, 1, COARSE)
    for j in BLK:
        for c in range(6):
            cst[c, j] = F[0, c, j, OWN, :]
        send(S_H + 8, cst, crecv, 1, j)

    hy = []
    for j in BLK:
        received(S_H + 8, cst, crecv, 1, j)

        @pl.when(tm == 0)
        def _():
            for c in range(6):
                yst[c, j] = rst[c, j]

        @pl.when(tm >= 1)
        def _():
            for c in range(6):
                yst[c, j] = rst[c, j] + crecv[c, j]

        hy += exchange(S_Y + 2 * j, yst.at[:, j, 0:8, :], yst.at[:, j, 8:16, :], HY.at[0, :, j], HY.at[1, :, j])
    for c in range(6):
        for j in BLK:
            F[0, c, j, OWN, :] = yst[c, j]
    for a in hy:
        a.wait()
    put_halo(HY)
    steps(8, 1, COARSE)
    for j in BLK:
        for c in range(6):
            est[c, j] = F[0, c, j, OWN, :]
        send(S_H + 12, est, erecv, 2, j)

    for j in BLK:
        received(S_H + 12, est, erecv, 2, j)

        @pl.when(tm < 2)
        def _():
            for c in range(6):
                corr[0, c, :, cols(j)] = brecv[c, j] + yst[c, j]

        @pl.when(tm >= 2)
        def _():
            for c in range(6):
                corr[0, c, :, cols(j)] = brecv[c, j] + (yst[c, j] + erecv[c, j])

    sent(S_H, bst, brecv, 1)
    sent(S_H + 4, ast, arecv, 2)
    sent(S_H + 8, cst, crecv, 1)
    sent(S_H + 12, est, erecv, 2)


def per_device(n_tm, n_space, cs, ini, bv, bs, bp, rr):
    vmem = pl.BlockSpec(memory_space=pltpu.VMEM)
    strip = pltpu.VMEM((6, BLOCKS, ROWS, 128), f32)
    halo8 = pltpu.VMEM((2, 6, BLOCKS, 8, 128), f32)
    shape = jax.ShapeDtypeStruct(cs.shape, f32)
    return pl.pallas_call(
        functools.partial(kernel, n_tm, n_space),
        out_shape=(shape, shape),
        in_specs=[pl.BlockSpec(memory_space=pl.ANY)] * 6,
        out_specs=(vmem, vmem),
        scratch_shapes=[
            pltpu.VMEM((2, 6, BLOCKS, HEIGHT, 128), f32),
            pltpu.VMEM((2, N_COEF, BLOCKS, HEIGHT, 128), f32),
            pltpu.VMEM((11, ROWS, 512), f32),
            pltpu.VMEM((2, 11, 8, 512), f32),
            halo8,
            pltpu.VMEM((2, 6, 2, 8, 128), f32),
            halo8,
            pltpu.VMEM((2, 6, 2, 8, 128), f32),
            strip, strip, strip, strip, strip, strip, strip, strip, strip, strip,
            pltpu.VMEM((6, ROWS, 512), f32),
            pltpu.SemaphoreType.DMA((32,)),
            pltpu.SemaphoreType.DMA((32,)),
            pltpu.SemaphoreType.DMA((6,)),
        ],
        compiler_params=pltpu.CompilerParams(
            collective_id=0, has_side_effects=True, vmem_limit_bytes=60 * 1024 * 1024
        ),
    )(cs, ini, bv, bs, bp, rr)


def solution(mesh):
    n_tm, n_space = mesh.shape["tm"], mesh.shape["space"]
    return jax.shard_map(
        functools.partial(per_device, n_tm, n_space),
        mesh=mesh,
        in_specs=(
            P("tm", None, "space", None),
            P(None, "space", None),
            P("space", None),
            P("space", None),
            P(None, "space", None),
            P("space", None),
        ),
        out_specs=(P("tm", None, "space", None), P("tm", None, "space", None)),
        check_vma=False,
    )
```

```python
import functools

import jax
import jax.numpy as jnp
from jax import lax
from jax.experimental import pallas as pl
from jax.experimental.pallas import tpu as pltpu
from jax.sharding import PartitionSpec as P

STEPS_SLAB = 8
FINE = 0.1
NU = 0.5
SOUND_SQ = 1.0
COARSE = STEPS_SLAB * FINE / 4.0

MESH = pl.DeviceIdType.MESH
f32 = jnp.float32

ROWS = 16
TOP = 16
HEIGHT = 48
BLOCKS = 4
N_COEF = 10


def kernel(
    n_tm, n_space,
    cs, ini, bv, bs, bp, rr,
    corr, resid,
    F, K, X, HX, HB, HR, HY, PR, bst, brecv, ast, arecv, rst, cst, crecv, yst, est, erecv,
    start_field, rbuf, cbuf, ssem, rsem, lsem,
):
    tm = lax.axis_index("tm")
    sp = lax.axis_index("space")
    up = lax.rem(sp + n_space - 1, n_space)
    down = lax.rem(sp + 1, n_space)

    def cols(j):
        return pl.ds(128 * j, 128)

    barrier = pltpu.get_barrier_semaphore()
    pl.semaphore_signal(barrier, inc=1, device_id={"space": up}, device_id_type=MESH)
    pl.semaphore_signal(barrier, inc=1, device_id={"space": down}, device_id_type=MESH)
    for d in (1, 2):
        @pl.when(tm >= d)
        def _():
            pl.semaphore_signal(barrier, inc=1, device_id={"tm": tm - d}, device_id_type=MESH)

    fetches = [
        pltpu.make_async_copy(src, dst, lsem.at[i])
        for i, (src, dst) in enumerate((
            (cs.at[0], X.at[0:6]), (bv, X.at[6]), (bs, X.at[7]), (bp, X.at[8:10]), (rr, X.at[10]), (ini, start_field),
        ))
    ]
    for a in fetches:
        a.start()

    zero8 = jnp.zeros((8, 128), f32)
    for b in range(2):
        for c in range(6):
            for j in range(BLOCKS):
                F[b, c, j, 0:8, :] = zero8
                F[b, c, j, 40:48, :] = zero8
    for b in range(2):
        for c in range(N_COEF):
            for j in range(BLOCKS):
                K[b, c, j, 0:8, :] = zero8
                K[b, c, j, 40:48, :] = zero8

    for a in fetches:
        a.wait()
    pl.semaphore_wait(barrier, 4 - tm // (n_tm - 1) - tm // (n_tm - 2))

    def exchange(i, to_up, to_down, from_up, from_down):
        a = pltpu.make_async_remote_copy(
            src_ref=to_up, dst_ref=from_down, send_sem=ssem.at[i], recv_sem=rsem.at[i],
            device_id={"space": up}, device_id_type=MESH)
        b = pltpu.make_async_remote_copy(
            src_ref=to_down, dst_ref=from_up, send_sem=ssem.at[i + 1], recv_sem=rsem.at[i + 1],
            device_id={"space": down}, device_id_type=MESH)
        a.start()
        b.start()
        return [a, b]

    def hop(i, src, dst, d, j):
        return pltpu.make_async_remote_copy(
            src_ref=src.at[:, j], dst_ref=dst.at[:, j], send_sem=ssem.at[i + j], recv_sem=rsem.at[i + j],
            device_id={"tm": lax.rem(tm + d, n_tm)}, device_id_type=MESH)

    def send(i, src, dst, d, j):
        @pl.when(tm + d < n_tm)
        def _():
            hop(i, src, dst, d, j).start()

    def sent(i, src, dst, d):
        @pl.when(tm + d < n_tm)
        def _():
            for j in range(BLOCKS):
                hop(i, src, dst, d, j).wait_send()

    def received(i, src, dst, d, j):
        @pl.when(tm >= d)
        def _():
            hop(i, src, dst, d, j).wait_recv()

    def set_coefs(rows, get):
        for j in range(BLOCKS):
            U, S, Pp, Q, R = [get(6 + i, j) for i in range(5)]
            for b, h in enumerate((FINE, COARSE)):
                k = 0.5 * h
                K[b, 0, j, rows, :] = k * U
                K[b, 1, j, rows, :] = h * S
                K[b, 2, j, rows, :] = (2.0 * h) * S
                K[b, 3, j, rows, :] = h * (Pp + R)
                K[b, 4, j, rows, :] = k * (Pp + R)
                K[b, 5, j, rows, :] = h * Q
                K[b, 6, j, rows, :] = k * Q
                K[b, 7, j, rows, :] = h * R
                K[b, 8, j, rows, :] = k * R
                K[b, 9, j, rows, :] = (1.0 - 4.0 * NU * h) - h * R

    def step(src, b, h, left, tiles):
        dst = 1 - src
        k = 0.5 * h
        c0 = 1.0 - 4.0 * NU * h
        c1 = NU * h
        lane = lax.broadcasted_iota(jnp.int32, (8, 128), 1)
        first = lane == 0
        last = lane == 127
        start = TOP - left

        def tile(t):
            r = start + 8 * t
            here = pl.ds(r, 8)
            cen, rm, rp = {}, {}, {}

            def center(c, j):
                if (c, j) not in cen:
                    cen[c, j] = F[src, c, j, here, :]
                return cen[c, j]

            def minus(c, j):
                if j < 0:
                    return zero8
                if (c, j) not in rm:
                    rm[c, j] = pltpu.roll(center(c, j), 1, 1)
                return rm[c, j]

            def plus(c, j):
                if j >= BLOCKS:
                    return zero8
                if (c, j) not in rp:
                    rp[c, j] = pltpu.roll(center(c, j), 127, 1)
                return rp[c, j]

            for j in range(BLOCKS):
                f, dx, dy, sm = [], [], [], []
                for c in range(6):
                    xm = F[src, c, j, pl.ds(r - 1, 8), :]
                    xp = F[src, c, j, pl.ds(r + 1, 8), :]
                    ym = jnp.where(first, minus(c, j - 1), minus(c, j))
                    yp = jnp.where(last, plus(c, j + 1), plus(c, j))
                    f.append(center(c, j))
                    dx.append(xp - xm)
                    dy.append(yp - ym)
                    sm.append((xp + xm) + (yp + ym))
                kU, hS, h2S, hPR, kPR, hQ, kQ, hR, kR, d0 = [K[b, i, j, here, :] for i in range(N_COEF)]
                div = dx[0] + dy[1]
                out = [
                    c0 * f[0] + c1 * sm[0] + k * (dx[3] - dx[2] + dy[4]) - kU * dx[0] - hS * f[1],
                    c0 * f[1] + c1 * sm[1] + k * (dx[4] - dy[2] + dy[5]) - kU * dx[1],
                    c0 * f[2] + c1 * sm[2] - (k * SOUND_SQ) * div,
                    d0 * f[3] + c1 * sm[3] - kU * dx[3] + h2S * f[4] + hPR * dx[0] + hQ * dy[0],
                    d0 * f[4] + c1 * sm[4] - kU * dx[4] + hS * f[5] + kQ * div + kPR * dx[1] + kR * dy[0],
                    d0 * f[5] + c1 * sm[5] - kU * dx[5] + hQ * dx[1] + hR * dy[1],
                ]
                for c in range(6):
                    F[dst, c, j, here, :] = out[c]

        for t in range(tiles):
            tile(t)

    def steps(count, b, h):
        def pairs(first, end, tiles):
            def pair(i, carry):
                step(0, b, h, count - 1 - 2 * i, tiles)
                step(1, b, h, count - 2 - 2 * i, tiles)
                return carry

            lax.fori_loop(first, end, pair, 0)

        if count > 4:
            pairs(0, (count - 4) // 2, 4)
        pairs((count - 4) // 2, count // 2, 3)

    def put_halo(buf):
        for c in range(6):
            for j in range(BLOCKS):
                F[0, c, j, 8:16, :] = buf[0, c, j]
                F[0, c, j, 32:40, :] = buf[1, c, j]

    OWN = slice(TOP, TOP + ROWS)

    BLK = range(BLOCKS)
    S_X, S_B, S_R, S_Y, S_H = 0, 8, 16, 20, 28

    hx = []
    for i, part in enumerate((slice(6, 9), slice(9, 11), slice(0, 3), slice(3, 6))):
        hx += exchange(S_X + 2 * i, X.at[part, 0:8, :], X.at[part, 8:16, :], HX.at[0, part], HX.at[1, part])
    for c in range(6):
        for j in BLK:
            F[0, c, j, OWN, :] = X[c, :, cols(j)]
    set_coefs(OWN, lambda i, j: X[i, :, cols(j)])
    halves = ((0, slice(8, 16)), (1, slice(32, 40)))
    for a in hx[:4]:
        a.wait()
    for side, rows in halves:
        set_coefs(rows, lambda i, j: HX[side, i, :, cols(j)])
    for a in hx[4:]:
        a.wait()
    for side, rows in halves:
        for c in range(6):
            for j in BLK:
                F[0, c, j, rows, :] = HX[side, c, :, cols(j)]
    steps(8, 0, FINE)

    hb = []
    for j in BLK:
        for c in range(6):
            bst[c, j] = F[0, c, j, OWN, :]
        hb += exchange(S_B + 2 * j, bst.at[:, j, 0:8, :], bst.at[:, j, 8:16, :], HB.at[0, :, j], HB.at[1, :, j])
    for j in BLK:
        send(S_H, bst, brecv, 1, j)
    for a in hb:
        a.wait()
    put_halo(HB)
    steps(8, 0, FINE)
    for j in BLK:
        for c in range(6):
            ast[c, j] = F[0, c, j, OWN, :]
        send(S_H + 4, ast, arecv, 2, j)

    hr = []
    for j in BLK:
        received(S_H, bst, brecv, 1, j)
        received(S_H + 4, ast, arecv, 2, j)

        @pl.when(tm == 0)
        def _():
            for c in range(6):
                brecv[c, j] = X[c, :, cols(j)]
                rst[c, j] = start_field[c, :, cols(j)] - X[c, :, cols(j)]

        @pl.when(tm == 1)
        def _():
            for c in range(6):
                rst[c, j] = brecv[c, j] - brecv[c, j]

        @pl.when(tm >= 2)
        def _():
            for c in range(6):
                rst[c, j] = arecv[c, j] - brecv[c, j]

        half = slice(4 * (j % 2), 4 * (j % 2) + 4)
        for c in range(6):
            PR[0, c, j // 2, half, :] = rst[c, j, 0:4, :]
            PR[1, c, j // 2, half, :] = rst[c, j, 12:16, :]
        if j % 2:
            p = j // 2
            hr += exchange(S_R + 2 * p, PR.at[0, :, p], PR.at[1, :, p], HR.at[0, :, p], HR.at[1, :, p])
    for c in range(6):
        for j in BLK:
            v = rst[c, j]
            rbuf[c, :, cols(j)] = v
            F[0, c, j, OWN, :] = v
    outs = [pltpu.make_async_copy(rbuf, resid.at[0], lsem.at[6])]
    outs[0].start()
    for a in hr:
        a.wait()
    for c in range(6):
        for j in BLK:
            half = slice(4 * (j % 2), 4 * (j % 2) + 4)
            F[0, c, j, 12:16, :] = HR[0, c, j // 2, half, :]
            F[0, c, j, 32:36, :] = HR[1, c, j // 2, half, :]
    steps(4, 1, COARSE)
    for j in BLK:
        for c in range(6):
            cst[c, j] = F[0, c, j, OWN, :]
        send(S_H + 8, cst, crecv, 1, j)

    hy = []
    for j in BLK:
        received(S_H + 8, cst, crecv, 1, j)

        @pl.when(tm == 0)
        def _():
            for c in range(6):
                yst[c, j] = rst[c, j]

        @pl.when(tm >= 1)
        def _():
            for c in range(6):
                yst[c, j] = rst[c, j] + crecv[c, j]

        hy += exchange(S_Y + 2 * j, yst.at[:, j, 0:8, :], yst.at[:, j, 8:16, :], HY.at[0, :, j], HY.at[1, :, j])
    for c in range(6):
        for j in BLK:
            F[0, c, j, OWN, :] = yst[c, j]
    for a in hy:
        a.wait()
    put_halo(HY)
    steps(8, 1, COARSE)
    for j in BLK:
        for c in range(6):
            est[c, j] = F[0, c, j, OWN, :]
        send(S_H + 12, est, erecv, 2, j)

    for j in BLK:
        received(S_H + 12, est, erecv, 2, j)

        @pl.when(tm < 2)
        def _():
            for c in range(6):
                cbuf[c, :, cols(j)] = brecv[c, j] + yst[c, j]

        @pl.when(tm >= 2)
        def _():
            for c in range(6):
                cbuf[c, :, cols(j)] = brecv[c, j] + (yst[c, j] + erecv[c, j])

        out = pltpu.make_async_copy(cbuf.at[:, :, cols(j)], corr.at[0, :, :, cols(j)], lsem.at[7 + j])
        out.start()
        outs.append(out)

    for a in outs:
        a.wait()
    sent(S_H, bst, brecv, 1)
    sent(S_H + 4, ast, arecv, 2)
    sent(S_H + 8, cst, crecv, 1)
    sent(S_H + 12, est, erecv, 2)


def per_device(n_tm, n_space, cs, ini, bv, bs, bp, rr):
    strip = pltpu.VMEM((6, BLOCKS, ROWS, 128), f32)
    halo8 = pltpu.VMEM((2, 6, BLOCKS, 8, 128), f32)
    shape = jax.ShapeDtypeStruct(cs.shape, f32)
    return pl.pallas_call(
        functools.partial(kernel, n_tm, n_space),
        out_shape=(shape, shape),
        in_specs=[pl.BlockSpec(memory_space=pl.ANY)] * 6,
        out_specs=(pl.BlockSpec(memory_space=pl.ANY),) * 2,
        scratch_shapes=[
            pltpu.VMEM((2, 6, BLOCKS, HEIGHT, 128), f32),
            pltpu.VMEM((2, N_COEF, BLOCKS, HEIGHT, 128), f32),
            pltpu.VMEM((11, ROWS, 512), f32),
            pltpu.VMEM((2, 11, 8, 512), f32),
            halo8,
            pltpu.VMEM((2, 6, 2, 8, 128), f32),
            halo8,
            pltpu.VMEM((2, 6, 2, 8, 128), f32),
            strip, strip, strip, strip, strip, strip, strip, strip, strip, strip,
            pltpu.VMEM((6, ROWS, 512), f32), pltpu.VMEM((6, ROWS, 512), f32), pltpu.VMEM((6, ROWS, 512), f32),
            pltpu.SemaphoreType.DMA((44,)),
            pltpu.SemaphoreType.DMA((44,)),
            pltpu.SemaphoreType.DMA((11,)),
        ],
        compiler_params=pltpu.CompilerParams(
            collective_id=0, has_side_effects=True, vmem_limit_bytes=60 * 1024 * 1024
        ),
    )(cs, ini, bv, bs, bp, rr)


def solution(mesh):
    n_tm, n_space = mesh.shape["tm"], mesh.shape["space"]
    return jax.shard_map(
        functools.partial(per_device, n_tm, n_space),
        mesh=mesh,
        in_specs=(
            P("tm", None, "space", None),
            P(None, "space", None),
            P("space", None),
            P("space", None),
            P(None, "space", None),
            P("space", None),
        ),
        out_specs=(P("tm", None, "space", None), P("tm", None, "space", None)),
        check_vma=False,
    )
```
